32 devices in a mesh: rows: 16 (over z, y, x), vars: 2 (over core).
Axes of the slice: x: 2, y: 2, z: 4, core: 2. Of those that a mesh axis runs over, the one named last changes fastest.
Arguments:
- fields: bfloat16 [16, 65536], P('vars', 'rows'), may hold values from -6 to 6
- stencil: int32 [32768, 4], P('rows'), may hold values from 0 to 1023
- stencil_weight: float32 [32768, 4], P('rows'), may hold values from 0.1 to 1
- owner_map: int32 [2048, 1], P('rows'), may hold values from 0 to 15; in each aligned block of 128 rows (0 to 127, 128 to 255, ...) at most 16 rows name the same one
- embed_weight: bfloat16 [16, 16, 1024], P('vars'), may hold values from -1.5 to 1.5
- embed_bias: bfloat16 [16, 1024], P('vars'), may hold values from -3 to 3
- agg_query: float32 [16, 64], replicated, may hold values from -40 to 40
- out_grad: bfloat16 [4096, 1024], P('rows'), may hold values from -6 to 6
Outputs:
- tokens: bfloat16 [4096, 1024], P('rows', 'vars')
- field_grad: float32 [16, 65536], P('vars', 'rows')
- weight_grad: float32 [16, 16, 1024], P('vars')
- bias_grad: float32 [16, 1024], P('vars')
- query_grad: float32 [16, 64], replicated
The draws below stay inside these ranges and needn't reach their ends.
Inputs may be any that keep to these rules, and one draw needn't show every extreme that they name: `stencil`: the index of a point within the pixel's own block. `owner_map`: among the 128 patches of one device along rows, no owner is named more than 16 times, a bound that some block reaches.
All inputs are finite; a program needn't handle non-finite values.
Results may differ from the reference program's by a relative error of at most 0.0055.
The reference program's roundings to bfloat16 on the way (of `matrix`, `pixels`, `embedded`, `grad_low` and `grad_pixels`) count: a program that leaves them out, or rounds other values in their place, can miss the bound.
Values may be sent and summed in bfloat16 or wider, within the bound.
A program may use at most 128 MiB of HBM per device.

```python
import math
import jax
import jax.numpy as jnp
import numpy as np
from jax import lax

D = 1024
H = 16
DH = 64
P_SIZE = 16
K = 4
NVAR = 16
PTS_BLK = 1024
PB = 32
BLOCKS = 4
PIX_BLK = 512
SRC = 128
MOST = 16
CAPR = 256
PATCHES = 2048
SLOTS = 4096
PIXELS = 32768
POINTS = 65536
N_ROWS = 16


def draw_agg_query(key, part):
    base = jax.random.normal(jax.random.fold_in(key, 11), (H, DH), jnp.float32)
    return jnp.clip(base, -4.5, 4.5)


def touch_ends(values, key, smallest, high):
    longest = values.shape.index(max(values.shape))
    spots = []
    for shift in (0, 1):
        where = [jax.random.randint(jax.random.fold_in(key, axis), (), 0, length) for axis, length in enumerate(values.shape)]
        where[longest] = (where[longest] + shift) % values.shape[longest]
        spots.append(tuple(where))
    return values.at[spots[0]].set(smallest).at[spots[1]].set(high)


def block_levels(stream_key, dims, split, low, top_value):
    loudness = 1.0
    for axis_at, blocks in split:
        heights = jax.random.uniform(jax.random.fold_in(jax.random.fold_in(stream_key, 6), axis_at), (blocks,), jnp.float32, low / len(split), top_value / len(split))
        loudness = loudness * jnp.repeat(jnp.exp(heights), dims[axis_at] // blocks).reshape((-1,) + (1,) * (len(dims) - 1 - axis_at))
    return loudness


def shared_out(rng, own, number, rows, count, top, limit, lean):
    ranking = jax.random.permutation(rng, count)
    packed, usual = portions_of(count, rows * top, limit, lean, True), portions_of(count, rows * top, limit, lean, False)
    places = jnp.arange(count)

    def named(sizes, turn):
        used = int((sizes > 0).sum())
        fixed = max(1, used // 4)
        shifted = fixed + (places - fixed + turn * (used - fixed)) % max(1, count - fixed)
        return jnp.zeros((count,), jnp.int32).at[ranking[jnp.where(places < fixed, places, shifted)]].set(jnp.asarray(sizes, jnp.int32))

    sizes = jnp.where(number % 4 == 0, named(packed, number // 4), named(usual, number - number // 4 - 1))
    mixed = jax.random.permutation(jax.random.fold_in(own, 3), count)
    donor, sink = mixed[0:count // 2 * 2:2], mixed[1:count // 2 * 2:2]
    slack = jnp.minimum(sizes[donor] - 1, limit - sizes[sink]) // 2
    slack = jnp.where((donor == ranking[0]) | (sink == ranking[0]) | (sizes[sink] == 0), 0, jnp.maximum(slack, 0))
    shifted = jax.random.randint(jax.random.fold_in(own, 4), (count // 2,), 0, 1 << 20) % (slack + 1)
    sizes = sizes.at[donor].add(-shifted).at[sink].add(shifted)
    labels = jnp.searchsorted(jnp.cumsum(sizes), jnp.arange(rows * top), side="right").astype(jnp.int32)
    listing = labels.reshape(top, rows).T
    listing = listing[jax.random.permutation(jax.random.fold_in(own, 1), rows)]
    turn = jax.random.randint(jax.random.fold_in(own, 2), (rows, 1), 0, top)
    return jnp.take_along_axis(listing, (jnp.arange(top)[None, :] + turn) % top, axis=1)


def portions_of(count, total, reach, skew, full):
    loads = [(1 << 20) // math.isqrt(grade ** skew) + 1 for grade in range(1, count + 1)]
    largest = reach if full else min(reach, max(-(-total // count), total * loads[0] // sum(loads)))
    least = 1 if total - largest >= count - 1 else 0
    given, surplus = [largest] + [least] * (count - 1), total - largest - least * (count - 1)
    while surplus > 0:
        free = [i for i in range(1, count) if given[i] < largest] or [i for i in range(1, count) if given[i] < reach]
        mass, left = sum([loads[i] for i in free]), surplus
        for i in free:
            addition = min(reach - given[i], max(1, left * loads[i] // mass), surplus)
            given[i] = given[i] + addition
            surplus = surplus - addition
    return np.array(given)


def noise(rng, extent, deviation, reach, shards=(), kind=jnp.bfloat16):
    level = block_levels(rng, extent, shards, -0.22, 0.18) if shards else 1.0
    values = jax.random.normal(rng, extent, jnp.float32) * deviation * level
    return jnp.minimum(jnp.maximum(values, -reach), reach).astype(kind)


def setup_inputs(seed: int = 0) -> dict:
    arg_keys = jax.random.split(jax.random.key(seed), 9)
    fields = noise(arg_keys[0], (NVAR, POINTS), 1.0, 6.0, ((0, 2), (1, 16)))
    stencil = touch_ends(jax.random.randint(arg_keys[1], (PIXELS, K), 0, PTS_BLK), jax.random.fold_in(arg_keys[1], 1), 0, PTS_BLK - 1).astype(jnp.int32)
    stencil_weight = jnp.clip(0.1 + 0.9 * jax.random.uniform(arg_keys[2], (PIXELS, K), jnp.float32) ** block_levels(arg_keys[2], (PIXELS, K), ((0, 16),), -0.2, 0.2), 0.1, 1.0)
    owner_map_keys = jax.random.split(jax.random.fold_in(arg_keys[3], 1), PATCHES // SRC)
    owner_map_turns = jax.random.permutation(jax.random.fold_in(arg_keys[3], 3), PATCHES // SRC)
    owner_map = jax.vmap(lambda own, number: shared_out(jax.random.fold_in(arg_keys[3], 2), own, number, SRC, N_ROWS, 1, MOST, 2))(owner_map_keys, owner_map_turns).reshape((PATCHES, 1))
    embed_weight = noise(arg_keys[4], (NVAR, P_SIZE, D), P_SIZE ** -0.5, 1.5, ((0, 2),))
    embed_bias = noise(arg_keys[5], (NVAR, D), 0.5, 3.0, ((0, 2),))
    agg_query = draw_agg_query(jax.random.fold_in(arg_keys[8], 71), 0)
    out_grad = noise(arg_keys[7], (SLOTS, D), 1.0, 6.0, ((0, 16),))
    return dict(fields=fields, stencil=stencil, stencil_weight=stencil_weight, owner_map=owner_map, embed_weight=embed_weight, embed_bias=embed_bias, agg_query=agg_query, out_grad=out_grad)


def interp_matrix(index_rows, weight_rows):
    columns = jnp.arange(PTS_BLK, dtype=jnp.int32)
    summed = jnp.zeros((index_rows.shape[0], PTS_BLK), jnp.float32)
    for entry in range(K):
        summed = summed + jnp.where(index_rows[:, entry:entry + 1] == columns[None, :], weight_rows[:, entry:entry + 1], 0.0)
    return summed.astype(jnp.bfloat16)

def reference(fields, stencil, stencil_weight, owner_map, embed_weight, embed_bias, agg_query, out_grad):
    high = lax.Precision.HIGHEST
    block_total = BLOCKS * N_ROWS
    field_blocks = fields.reshape(NVAR, block_total, PTS_BLK).transpose(1, 0, 2)
    index_blocks = stencil.reshape(block_total, PIX_BLK, K)
    weight_blocks = stencil_weight.reshape(block_total, PIX_BLK, K)

    def forward_block(pieces):
        field_block, index_rows, weight_rows = pieces
        matrix = interp_matrix(index_rows, weight_rows)
        return jnp.dot(field_block, matrix.T, preferred_element_type=jnp.float32).astype(jnp.bfloat16)
    pixels = lax.map(forward_block, (field_blocks, index_blocks, weight_blocks))
    pixels = pixels.reshape(N_ROWS, BLOCKS, NVAR, PB, P_SIZE).transpose(0, 1, 3, 2, 4).reshape(N_ROWS, SRC, NVAR, P_SIZE)
    routes = owner_map.reshape(N_ROWS, SRC)
    onehot = (routes[:, :, None] == jnp.arange(N_ROWS, dtype=jnp.int32)[None, None, :]).astype(jnp.int32)
    order_rank = lax.optimization_barrier(jnp.sum(onehot * (jnp.cumsum(onehot, axis=1) - 1), axis=2))
    slots = routes * CAPR + jnp.arange(N_ROWS, dtype=jnp.int32)[:, None] * MOST + order_rank
    slots = slots.astype(jnp.int32)
    upstream_all = out_grad[slots.reshape(-1)].reshape(N_ROWS, SRC, D)
    score_scale = 1.0 / math.sqrt(DH)
    query_f = agg_query.astype(jnp.float32)
    weight_f = embed_weight.astype(jnp.float32)
    bias_f = embed_bias.astype(jnp.float32)

    def owner_step(running, pieces):
        weight_acc, bias_acc, query_acc = running
        pix_rows, grad_rows = pieces
        embedded = (jnp.einsum('svp,vpd->svd', pix_rows.astype(jnp.float32), weight_f, precision=high) + bias_f[None]).astype(jnp.bfloat16)
        head_view = embedded.astype(jnp.float32).reshape(SRC, NVAR, H, DH)
        scores = jnp.einsum('svhe,he->shv', head_view, query_f, precision=high) * score_scale
        attention = jax.nn.softmax(scores, axis=2)
        mixture = jnp.einsum('shv,svhe->she', attention, head_view, precision=high)
        token_rows = mixture.reshape(SRC, D).astype(jnp.bfloat16)
        upstream = grad_rows.astype(jnp.float32).reshape(SRC, H, DH)
        inner_out = lax.optimization_barrier(jnp.sum(upstream * mixture, axis=2))
        grad_attn = jnp.einsum('she,svhe->shv', upstream, head_view, precision=high)
        grad_score = attention * (grad_attn - inner_out[:, :, None])
        grad_embed = jnp.einsum('shv,she->svhe', attention, upstream, precision=high) + jnp.einsum('shv,he->svhe', grad_score, query_f, precision=high) * score_scale
        grad_embed = grad_embed.reshape(SRC, NVAR, D)
        grad_low = grad_embed.astype(jnp.bfloat16)
        weight_acc = weight_acc + jnp.einsum('svp,svd->vpd', pix_rows.astype(jnp.float32), grad_low.astype(jnp.float32), precision=high)
        bias_acc = bias_acc + lax.optimization_barrier(jnp.sum(grad_embed, axis=0))
        query_acc = query_acc + jnp.einsum('shv,svhe->he', grad_score, head_view, precision=high) * score_scale
        grad_pixels = jnp.einsum('svd,vpd->svp', grad_low.astype(jnp.float32), weight_f, precision=high).astype(jnp.bfloat16)
        return ((weight_acc, bias_acc, query_acc), (token_rows, grad_pixels))
    start_sums = (jnp.zeros((NVAR, P_SIZE, D), jnp.float32), jnp.zeros((NVAR, D), jnp.float32), jnp.zeros((H, DH), jnp.float32))
    sums_final, outputs = lax.scan(owner_step, start_sums, (pixels, upstream_all))
    weight_grad, bias_grad, query_grad = sums_final
    token_rows, grad_pixels = outputs
    tokens = jnp.zeros((SLOTS, D), jnp.bfloat16).at[slots.reshape(-1)].set(token_rows.reshape(PATCHES, D))
    grad_blocks = grad_pixels.reshape(N_ROWS, BLOCKS, PB, NVAR, P_SIZE).transpose(0, 1, 3, 2, 4).reshape(block_total, NVAR, PIX_BLK)

    def backward_block(pieces):
        grad_block, index_rows, weight_rows = pieces
        matrix = interp_matrix(index_rows, weight_rows)
        return jnp.dot(grad_block, matrix, preferred_element_type=jnp.float32)
    field_blocks_grad = lax.map(backward_block, (grad_blocks, index_blocks, weight_blocks))
    field_grad = field_blocks_grad.transpose(1, 0, 2).reshape(NVAR, POINTS)
    return (tokens, field_grad, weight_grad, bias_grad, query_grad)
```

```python
import functools
import math

import jax
import jax.numpy as jnp
from jax import lax
from jax.experimental import pallas as pl
from jax.experimental.pallas import tpu as pltpu
from jax.sharding import PartitionSpec as P

D = 1024
H = 16
DH = 64
P_SIZE = 16
K = 4
PTS_BLK = 1024
PB = 32
LANE = 128
SUB = 8
J_STEP = 64
MESH = pl.DeviceIdType.MESH
F32 = jnp.float32
BF16 = jnp.bfloat16


def nn(a, b):
    return lax.dot_general(a, b, (((1,), (0,)), ((), ())), preferred_element_type=F32)


def nt(a, b):
    return lax.dot_general(a, b, (((1,), (1,)), ((), ())), preferred_element_type=F32)


def iota(shape, axis):
    return lax.broadcasted_iota(jnp.int32, shape, axis)


def split_two(x):
    high = x.astype(BF16)
    return high, (x - high.astype(F32)).astype(BF16)


def expand(x, spread):
    high, low = split_two(x)
    return nn(high, spread) + nn(low, spread)


def aligned(start, size):
    return pl.ds(pl.multiple_of(start * size, size), size)


def kernel(
    n_rows, n_vars, var_local, blocks, depth,
    fields, stencil, stencil_weight, owner_col, owner_row, weight, bias, query, out_grad,
    tok_out, field_out, weight_out, bias_out, query_out,
    arrived, matrix, spread_fields, up, pix_t, emb, scores, attn_grad,
    mix_send, mix_recv, stat, tok_send, bias_sum, query_part, part_send, part_recv,
    small_send, small_recv, done,
    og_s, og_r, sw_s, sw_r, mx_s, mx_r, st_s, st_r, tk_s, tk_r, qp_s, qp_r,
    pt_s, pt_r, sm_s, sm_r, dn_s, dn_r,
):
    me = lax.axis_index("rows")
    mine = lax.axis_index("vars")
    patches = blocks * PB
    vp = var_local * P_SIZE
    width = D // n_vars
    slots = n_rows * depth
    block_pixels = PB * P_SIZE
    scale = 1.0 / math.sqrt(DH)
    tiles = vp // SUB * (D // LANE) // n_rows

    def row_dev(peer):
        return (peer, mine)

    def var_dev(peer):
        return (me, peer)

    def copy(src, dst, send, recv, device):
        return pltpu.make_async_remote_copy(
            src_ref=src, dst_ref=dst, send_sem=send, recv_sem=recv,
            device_id=device, device_id_type=MESH,
        )

    def each_row(body):
        def step(i, carry):
            body(lax.rem(me + i, n_rows))
            return carry

        lax.fori_loop(1, n_rows, step, 0)

    def each_var(body):
        for i in range(1, n_vars):
            body(lax.rem(mine + i, n_vars))

    barrier = pltpu.get_barrier_semaphore()
    each_row(
        lambda p: pl.semaphore_signal(barrier, inc=1, device_id=row_dev(p), device_id_type=MESH)
    )
    each_var(
        lambda p: pl.semaphore_signal(barrier, inc=1, device_id=var_dev(p), device_id_type=MESH)
    )
    pl.semaphore_wait(barrier, n_rows + n_vars - 2)

    own_lanes = pl.ds(pl.multiple_of(mine * width, LANE), width)

    def og_copy(src_row, dst_row, send, recv, p):
        return copy(
            out_grad.at[aligned(src_row, depth), own_lanes],
            arrived.at[mine, aligned(dst_row, depth), :],
            og_s.at[send], og_r.at[recv], row_dev(p),
        )

    each_row(lambda p: og_copy(p, me, p, me, p).start())
    arrived[mine, aligned(me, depth), :] = out_grad[aligned(me, depth), own_lanes]

    def own_pixel(shape, row_axis):
        return iota(shape, 0) % P_SIZE == iota(shape, 1) % P_SIZE

    def placing(b):
        shape = (patches, block_pixels)
        return (iota(shape, 0) == b * PB + iota(shape, 1) // P_SIZE).astype(F32).astype(BF16)

    def interp(b, pix):
        columns = aligned(b, block_pixels)
        index_rows = stencil[:, columns]
        weight_rows = stencil_weight[:, columns]

        def chunk(j, carry):
            points = j * J_STEP + iota((J_STEP, block_pixels), 0)
            total = jnp.zeros((J_STEP, block_pixels), F32)
            for entry in range(K):
                total = total + jnp.where(
                    index_rows[entry : entry + 1] == points,
                    weight_rows[entry : entry + 1],
                    0.0,
                )
            matrix[b, aligned(j, J_STEP), :] = total.astype(BF16)
            return carry

        lax.fori_loop(0, PTS_BLK // J_STEP, chunk, 0)
        block_fields = fields[:, aligned(b, PTS_BLK)].astype(F32)
        for v in range(var_local):
            spread_fields[v * P_SIZE : (v + 1) * P_SIZE, :] = jnp.broadcast_to(
                block_fields[v : v + 1], (P_SIZE, PTS_BLK)
            ).astype(BF16)
        values = nn(spread_fields[...], matrix[b]).astype(BF16).astype(F32)
        kept = jnp.where(own_pixel((vp, block_pixels), 0), values, 0.0).astype(BF16)
        return pix + nt(placing(b), kept)

    pix = lax.fori_loop(0, blocks, interp, jnp.zeros((patches, vp), F32))
    pix_t[...] = pix.T.astype(BF16)

    square = (patches, patches)
    same = owner_col[...] == owner_row[...]
    rank_col = jnp.sum(
        jnp.where(same & (iota(square, 1) < iota(square, 0)), 1.0, 0.0), axis=1, keepdims=True
    ).astype(jnp.int32)
    rank_row = jnp.sum(
        jnp.where(same & (iota(square, 0) < iota(square, 1)), 1.0, 0.0), axis=0, keepdims=True
    ).astype(jnp.int32)
    slot_col = owner_col[...] * depth + rank_col
    slot_row = owner_row[...] * depth + rank_row
    take = (slot_col == iota((patches, slots), 1)).astype(F32).astype(BF16)
    put = (slot_row == iota((slots, patches), 0)).astype(F32).astype(BF16)

    each_row(lambda p: og_copy(p, p, p, p, p).wait_recv())

    def swap_copy(part, sem_s, sem_r, p):
        return copy(arrived.at[part], arrived.at[part], sw_s.at[sem_s], sw_r.at[sem_r], var_dev(p))

    each_var(lambda p: swap_copy(mine, p, mine, p).start())

    heads = iota((H, D), 0) == iota((H, D), 1) // DH
    spread = heads.astype(F32).astype(BF16)
    own_heads = iota((H, width), 0) == (mine * width + iota((H, width), 1)) // DH
    own_spread = own_heads.astype(F32).astype(BF16)
    query_wide = jnp.where(heads, query[...], 0.0)
    query_a = query_wide.astype(BF16)
    rest = query_wide - query_a.astype(F32)
    query_b = rest.astype(BF16)
    query_c = (rest - query_b.astype(F32)).astype(BF16)

    def embed(v, carry):
        mask = iota((patches, vp), 1) // P_SIZE == v
        own = jnp.where(mask, pix, 0.0).astype(BF16)
        low = (nn(own, weight[...]) + bias[pl.ds(v, 1), :]).astype(BF16)
        emb[v] = low
        scores[v] = (nt(low, query_a) + nt(low, query_b) + nt(low, query_c)) * scale
        return carry

    lax.fori_loop(0, var_local, embed, 0)
    each_var(lambda p: swap_copy(p, p, p, p).wait_recv())
    for part in range(n_vars):
        up[:, part * width : (part + 1) * width] = nn(take, arrived[part])

    peak = jnp.max(scores[...], axis=0)

    def gather(v, carry):
        total, inner, mixed = carry
        values = emb[v].astype(F32)
        high, low = split_two(up[...] * values)
        grad = nt(high, spread) + nt(low, spread)
        attn_grad[v] = grad
        power = jnp.exp(scores[v] - peak)
        scores[v] = power
        return total + power, inner + power * grad, mixed + expand(power, spread) * values

    nothing = jnp.zeros((patches, H), F32)
    total, inner, mixed = lax.fori_loop(
        0, var_local, gather, (nothing, nothing, jnp.zeros((patches, D), F32))
    )
    stat[mine, 0] = peak
    stat[mine, 1] = total
    stat[mine, 2] = inner
    for part in range(n_vars):
        mix_send[part] = mixed[:, part * width : (part + 1) * width]

    def stat_copy(part, sem_s, sem_r, p):
        return copy(stat.at[part], stat.at[part], st_s.at[sem_s], st_r.at[sem_r], var_dev(p))

    def mix_copy(part, slot, sem_s, sem_r, p):
        return copy(
            mix_send.at[part], mix_recv.at[slot], mx_s.at[sem_s], mx_r.at[sem_r], var_dev(p)
        )

    each_var(lambda p: stat_copy(mine, p, mine, p).start())
    each_var(lambda p: mix_copy(p, mine, p, mine, p).start())
    mix_recv[mine] = mix_send[mine]
    each_var(lambda p: stat_copy(p, p, p, p).wait_recv())
    peak_all = stat[0, 0]
    for part in range(1, n_vars):
        peak_all = jnp.maximum(peak_all, stat[part, 0])
    factors = [jnp.exp(stat[part, 0] - peak_all) for part in range(n_vars)]
    total_all = sum(stat[part, 1] * factors[part] for part in range(n_vars))
    inner_all = sum(stat[part, 2] * factors[part] for part in range(n_vars)) / total_all
    own_factor = jnp.exp(peak - peak_all) / total_all

    each_var(lambda p: mix_copy(p, p, p, p, p).wait_recv())
    mixture = sum(
        expand(factors[part] / total_all, own_spread) * mix_recv[part] for part in range(n_vars)
    )
    tok_send[...] = nn(put, mixture.astype(BF16)).astype(BF16)

    def tok_copy(src_row, dst_row, send, recv, p):
        return copy(
            tok_send.at[aligned(src_row, depth), :], tok_out.at[aligned(dst_row, depth), :],
            tk_s.at[send], tk_r.at[recv], row_dev(p),
        )

    each_row(lambda p: tok_copy(p, me, p, me, p).start())
    tok_out[aligned(me, depth), :] = tok_send[aligned(me, depth), :]

    query_scaled = query[...] * scale

    def part_copy(slot_s, slot_r, send, recv, p):
        return copy(
            part_send.at[slot_s], part_recv.at[slot_r], pt_s.at[send], pt_r.at[recv], row_dev(p)
        )

    per_group = D // LANE // tiles
    per_var = P_SIZE // SUB * per_group

    def backward(i, carry):
        pix_grad, query_sum = carry
        v = lax.rem(i + me // per_var, var_local)
        values = emb[v].astype(F32)
        attention = scores[v] * own_factor
        score_grad = attention * (attn_grad[v] - inner_all)
        score_wide = expand(score_grad, spread)
        grad = expand(attention, spread) * up[...] + score_wide * query_scaled
        low = grad.astype(BF16)
        bias_sum[v] = jnp.sum(grad, axis=0, keepdims=True)
        query_sum = query_sum + jnp.sum(score_wide * values, axis=0, keepdims=True)
        found = nn(pix_t[aligned(v, P_SIZE), :], low)
        for group in range(P_SIZE // SUB):
            for lane in range(D // LANE):
                slot = v * per_var + group * per_group + lane // tiles
                part_send[slot, lane % tiles] = found[
                    group * SUB : (group + 1) * SUB, lane * LANE : (lane + 1) * LANE
                ]
        for step in range(per_var):
            slot = v * per_var + step

            @pl.when(slot != me)
            def _():
                part_copy(slot, me, slot, me, slot).start()

        mask = iota((patches, vp), 1) // P_SIZE == v
        pix_grad = pix_grad + jnp.where(mask, nt(low, weight[...]), 0.0)
        return pix_grad, query_sum

    pix_grad, query_sum = lax.fori_loop(
        0, var_local, backward, (jnp.zeros((patches, vp), F32), jnp.zeros((1, D), F32))
    )
    part_recv[me] = part_send[me]

    query_part[mine] = jnp.broadcast_to(query_sum * scale, (SUB, D))

    def query_copy(part, sem_s, sem_r, p):
        return copy(
            query_part.at[part], query_part.at[part], qp_s.at[sem_s], qp_r.at[sem_r], var_dev(p)
        )

    each_var(lambda p: query_copy(mine, p, mine, p).start())

    grad_t = pix_grad.T.astype(BF16)
    pick = (iota((var_local, vp), 0) == iota((var_local, vp), 1) // P_SIZE).astype(F32).astype(BF16)

    small_send[...] = jnp.zeros_like(small_send)
    bias_tiles = var_local // SUB * (D // LANE)
    for group in range(var_local // SUB):
        rows = jnp.concatenate([bias_sum[group * SUB + k] for k in range(SUB)], axis=0)
        for lane in range(D // LANE):
            small_send[group * (D // LANE) + lane] = rows[:, lane * LANE : (lane + 1) * LANE]
    each_var(lambda p: query_copy(p, p, p, p).wait_recv())
    query_all = query_part[0]
    for part in range(1, n_vars):
        query_all = query_all + query_part[part]
    for lane in range(D // LANE):
        small_send[bias_tiles + lane] = query_all[:, lane * LANE : (lane + 1) * LANE]

    def small_copy(slot_s, slot_r, send, recv, p):
        return copy(
            small_send.at[slot_s], small_recv.at[slot_r], sm_s.at[send], sm_r.at[recv], row_dev(p)
        )

    each_row(lambda p: small_copy(p, me, p, me, p).start())
    small_recv[me] = small_send[me]

    def field_block(b, carry):
        values = nn(grad_t, placing(b))
        kept = jnp.where(own_pixel((vp, block_pixels), 0), values, 0.0).astype(BF16)
        by_pixel = nn(pick, kept).astype(BF16)
        field_out[:, aligned(b, PTS_BLK)] = nt(by_pixel, matrix[b])
        return carry

    lax.fori_loop(0, blocks, field_block, 0)

    each_row(lambda p: part_copy(p, p, p, p, p).wait_recv())
    each_row(lambda p: small_copy(p, p, p, p, p).wait_recv())
    done[me, 0:tiles] = jnp.sum(part_recv[...], axis=0)
    done[me, tiles] = jnp.sum(small_recv[...], axis=0)

    def done_copy(slot, send, recv, p):
        return copy(done.at[slot], done.at[slot], dn_s.at[send], dn_r.at[recv], row_dev(p))

    each_row(lambda p: done_copy(me, p, me, p).start())
    each_row(lambda p: done_copy(p, p, p, p).wait_recv())
    for slot in range(n_rows):
        for tile in range(tiles):
            number = slot * tiles + tile
            group, lane = number // (D // LANE), number % (D // LANE)
            weight_out[group * SUB : (group + 1) * SUB, lane * LANE : (lane + 1) * LANE] = done[
                slot, tile
            ]
    for number in range(bias_tiles):
        group, lane = number // (D // LANE), number % (D // LANE)
        bias_out[group * SUB : (group + 1) * SUB, lane * LANE : (lane + 1) * LANE] = done[
            number, tiles
        ]
    for lane in range(D // LANE):
        query_out[:, lane * LANE : (lane + 1) * LANE] = done[bias_tiles + lane, tiles]

    each_row(lambda p: tok_copy(p, p, p, p, p).wait_recv())
    each_row(lambda p: og_copy(p, me, p, me, p).wait_send())
    each_row(lambda p: tok_copy(p, me, p, me, p).wait_send())
    each_row(lambda p: part_copy(p, me, p, me, p).wait_send())
    each_row(lambda p: small_copy(p, me, p, me, p).wait_send())
    each_row(lambda p: done_copy(me, p, me, p).wait_send())
    each_var(lambda p: swap_copy(mine, p, mine, p).wait_send())
    each_var(lambda p: stat_copy(mine, p, mine, p).wait_send())
    each_var(lambda p: mix_copy(p, mine, p, mine, p).wait_send())
    each_var(lambda p: query_copy(mine, p, mine, p).wait_send())


def local(
    fields, stencil, stencil_weight, owner_map, embed_weight, embed_bias, agg_query, out_grad
):
    n_rows = lax.axis_size("rows")
    n_vars = lax.axis_size("vars")
    var_local, points = fields.shape
    blocks = points // PTS_BLK
    patches = owner_map.shape[0]
    capacity = out_grad.shape[0]
    slot_depth = capacity // n_rows
    depth = -(-slot_depth // 16) * 16
    vp = var_local * P_SIZE
    width = D // n_vars
    slots = n_rows * depth
    tiles = vp // SUB * (D // LANE) // n_rows
    if depth != slot_depth:
        out_grad = jnp.pad(
            out_grad.reshape(n_rows, slot_depth, D), ((0, 0), (0, depth - slot_depth), (0, 0))
        ).reshape(slots, D)
    vmem = pl.BlockSpec(memory_space=pltpu.VMEM)
    dma = pltpu.SemaphoreType.DMA
    row_sem, var_sem = dma((n_rows,)), dma((n_vars,))
    tokens, field_grad, weight_grad, bias_grad, query_grad = pl.pallas_call(
        functools.partial(kernel, n_rows, n_vars, var_local, blocks, depth),
        out_shape=(
            jax.ShapeDtypeStruct((slots, width), BF16),
            jax.ShapeDtypeStruct((var_local, points), F32),
            jax.ShapeDtypeStruct((vp, D), F32),
            jax.ShapeDtypeStruct((var_local, D), F32),
            jax.ShapeDtypeStruct((SUB, D), F32),
        ),
        in_specs=[vmem] * 9,
        out_specs=(vmem,) * 5,
        scratch_shapes=[
            pltpu.VMEM((n_vars, slots, width), BF16),
            pltpu.VMEM((blocks, PTS_BLK, PB * P_SIZE), BF16),
            pltpu.VMEM((vp, PTS_BLK), BF16),
            pltpu.VMEM((patches, D), F32),
            pltpu.VMEM((vp, patches), BF16),
            pltpu.VMEM((var_local, patches, D), BF16),
            pltpu.VMEM((var_local, patches, H), F32),
            pltpu.VMEM((var_local, patches, H), F32),
            pltpu.VMEM((n_vars, patches, width), F32),
            pltpu.VMEM((n_vars, patches, width), F32),
            pltpu.VMEM((n_vars, 3, patches, H), F32),
            pltpu.VMEM((slots, width), BF16),
            pltpu.VMEM((var_local, 1, D), F32),
            pltpu.VMEM((n_vars, SUB, D), F32),
            pltpu.VMEM((n_rows, tiles, SUB, LANE), F32),
            pltpu.VMEM((n_rows, tiles, SUB, LANE), F32),
            pltpu.VMEM((n_rows, SUB, LANE), F32),
            pltpu.VMEM((n_rows, SUB, LANE), F32),
            pltpu.VMEM((n_rows, tiles + 1, SUB, LANE), F32),
        ]
        + [row_sem] * 2 + [var_sem] * 6 + [row_sem] * 2 + [var_sem] * 2 + [row_sem] * 6,
        compiler_params=pltpu.CompilerParams(
            collective_id=0, has_side_effects=True, vmem_limit_bytes=48 * 1024 * 1024
        ),
        name="encoder",
    )(
        fields,
        stencil.T,
        stencil_weight.T,
        owner_map,
        owner_map.reshape(1, patches),
        embed_weight.reshape(vp, D),
        embed_bias.astype(F32),
        agg_query.reshape(1, D),
        out_grad,
    )
    if depth != slot_depth:
        tokens = tokens.reshape(n_rows, depth, width)[:, :slot_depth].reshape(capacity, width)
    return (
        tokens,
        field_grad,
        weight_grad.reshape(var_local, P_SIZE, D),
        bias_grad,
        query_grad[0].reshape(H, DH),
    )


def solution(mesh):
    return jax.shard_map(
        local,
        mesh=mesh,
        in_specs=(
            P("vars", "rows"),
            P("rows", None),
            P("rows", None),
            P("rows", None),
            P("vars", None, None),
            P("vars", None),
            P(),
            P("rows", None),
        ),
        out_specs=(
            P("rows", "vars"),
            P("vars", "rows"),
            P("vars", None, None),
            P("vars", None),
            P(),
        ),
        check_vma=False,
    )
```

```python
import functools
import math

import jax
import jax.numpy as jnp
from jax import lax
from jax.experimental import pallas as pl
from jax.experimental.pallas import tpu as pltpu
from jax.sharding import PartitionSpec as P

D = 1024
H = 16
DH = 64
P_SIZE = 16
K = 4
PTS_BLK = 1024
PB = 32
LANE = 128
SUB = 8
J_STEP = 64
PLANE = 4
PAIR = 2
COPIES = 2 * H
MESH = pl.DeviceIdType.MESH
F32 = jnp.float32
BF16 = jnp.bfloat16


def nn(a, b):
    return lax.dot_general(a, b, (((1,), (0,)), ((), ())), preferred_element_type=F32)


def nt(a, b):
    return lax.dot_general(a, b, (((1,), (1,)), ((), ())), preferred_element_type=F32)


def iota(shape, axis):
    return lax.broadcasted_iota(jnp.int32, shape, axis)


def split_two(x):
    high = x.astype(BF16)
    return high, (x - high.astype(F32)).astype(BF16)


def expand(x, spread):
    high = x.astype(BF16).astype(F32)
    return nn(jnp.where(iota(x.shape, 1) < H, high, x - high).astype(BF16), spread)


def aligned(start, size):
    return pl.ds(pl.multiple_of(start * size, size), size)


def kernel(
    n_rows, n_vars, var_local, blocks, depth,
    fields, stencil, stencil_weight, owner_col, owner_row, weight, bias, query, out_grad,
    tok_out, field_out, done,
    weight_in, arrived, matrix, spread_fields, up, pix_t, emb, bias_wide, scores, attn_grad,
    mix_send, mix_recv, stat, tok_send, bias_sum, query_part, part_send, part_recv,
    small_send, small_recv, plane_sum, line_recv,
    og_s, og_r, sw_s, sw_r, mx_s, mx_r, st_s, st_r, tk_s, tk_r, qp_s, qp_r,
    pt_s, pt_r, sm_s, sm_r, ln_s, ln_r, up_s, up_r, dn_s, dn_r, load_sem,
):
    me = lax.axis_index("rows")
    mine = lax.axis_index("vars")
    lines = n_rows // PLANE
    my_line, my_place = me // PLANE, lax.rem(me, PLANE)
    patches = blocks * PB
    vp = var_local * P_SIZE
    width = D // n_vars
    slots = n_rows * depth
    block_pixels = PB * P_SIZE
    scale = 1.0 / math.sqrt(DH)
    tiles = vp // SUB * (D // LANE) // n_rows

    def row_dev(peer):
        return (peer, mine)

    def var_dev(peer):
        return (me, peer)

    def copy(src, dst, send, recv, device):
        return pltpu.make_async_remote_copy(
            src_ref=src, dst_ref=dst, send_sem=send, recv_sem=recv,
            device_id=device, device_id_type=MESH,
        )

    def each_row(body):
        def step(i, carry):
            body(lax.rem(me + i, n_rows))
            return carry

        lax.fori_loop(1, n_rows, step, 0)

    def each_var(body):
        for i in range(1, n_vars):
            body(lax.rem(mine + i, n_vars))

    def each_place(body):
        for i in range(1, PLANE):
            body(lax.rem(my_place + i, PLANE))

    def each_line(body):
        for i in range(1, lines):
            body(lax.rem(my_line + i, lines))

    own_lanes = pl.ds(pl.multiple_of(mine * width, LANE), width)
    weight_load = pltpu.make_async_copy(weight, weight_in, load_sem.at[0])
    weight_load.start()
    own_load = pltpu.make_async_copy(
        out_grad.at[aligned(me, depth), own_lanes],
        arrived.at[mine, aligned(me, depth), :],
        load_sem.at[1],
    )
    own_load.start()
    barrier = pltpu.get_barrier_semaphore()
    each_row(
        lambda p: pl.semaphore_signal(barrier, inc=1, device_id=row_dev(p), device_id_type=MESH)
    )
    each_var(
        lambda p: pl.semaphore_signal(barrier, inc=1, device_id=var_dev(p), device_id_type=MESH)
    )
    pl.semaphore_wait(barrier, n_rows + n_vars - 2)

    def og_copy(src_row, dst_row, send, recv, p):
        return copy(
            out_grad.at[aligned(src_row, depth), own_lanes],
            arrived.at[mine, aligned(dst_row, depth), :],
            og_s.at[send], og_r.at[recv], row_dev(p),
        )

    each_row(lambda p: og_copy(p, me, p, me, p).start())

    def own_pixel(shape, row_axis):
        return iota(shape, 0) % P_SIZE == iota(shape, 1) % P_SIZE

    def placing(b):
        shape = (patches, block_pixels)
        return (iota(shape, 0) == b * PB + iota(shape, 1) // P_SIZE).astype(F32).astype(BF16)

    def interp(b, pix):
        columns = aligned(b, block_pixels)
        index_rows = stencil[:, columns]
        weight_rows = stencil_weight[:, columns]

        def chunk(j, carry):
            points = j * J_STEP + iota((J_STEP, block_pixels), 0)
            total = jnp.zeros((J_STEP, block_pixels), F32)
            for entry in range(K):
                total = total + jnp.where(
                    index_rows[entry : entry + 1] == points,
                    weight_rows[entry : entry + 1],
                    0.0,
                )
            matrix[b, aligned(j, J_STEP), :] = total.astype(BF16)
            return carry

        lax.fori_loop(0, PTS_BLK // J_STEP, chunk, 0)
        block_fields = fields[:, aligned(b, PTS_BLK)].astype(F32)
        for v in range(var_local):
            spread_fields[v * P_SIZE : (v + 1) * P_SIZE, :] = jnp.broadcast_to(
                block_fields[v : v + 1], (P_SIZE, PTS_BLK)
            ).astype(BF16)
        values = nn(spread_fields[...], matrix[b]).astype(BF16).astype(F32)
        kept = jnp.where(own_pixel((vp, block_pixels), 0), values, 0.0).astype(BF16)
        return pix + nt(placing(b), kept)

    pix = lax.fori_loop(0, blocks, interp, jnp.zeros((patches, vp), F32))
    pix_t[...] = pix.T.astype(BF16)

    square = (patches, patches)
    same = owner_col[...] == owner_row[...]
    rank_col = jnp.sum(
        jnp.where(same & (iota(square, 1) < iota(square, 0)), 1.0, 0.0), axis=1, keepdims=True
    ).astype(jnp.int32)
    rank_row = jnp.sum(
        jnp.where(same & (iota(square, 0) < iota(square, 1)), 1.0, 0.0), axis=0, keepdims=True
    ).astype(jnp.int32)
    slot_col = owner_col[...] * depth + rank_col
    slot_row = owner_row[...] * depth + rank_row
    take = (slot_col == iota((patches, slots), 1)).astype(F32).astype(BF16)
    put = (slot_row == iota((slots, patches), 0)).astype(F32).astype(BF16)

    own_load.wait()
    each_row(lambda p: og_copy(p, p, p, p, p).wait_recv())

    def swap_copy(part, sem_s, sem_r, p):
        return copy(arrived.at[part], arrived.at[part], sw_s.at[sem_s], sw_r.at[sem_r], var_dev(p))

    each_var(lambda p: swap_copy(mine, p, mine, p).start())

    heads = iota((COPIES, D), 0) % H == iota((COPIES, D), 1) // DH
    spread = heads.astype(F32).astype(BF16)
    own_head = (mine * width + iota((COPIES, width), 1)) // DH
    own_spread = (iota((COPIES, width), 0) % H == own_head).astype(F32).astype(BF16)
    query_tiled = jnp.concatenate([query[...]] * H, axis=1)
    query_wide = jnp.where(heads, jnp.concatenate([query_tiled] * 2, axis=0), 0.0)
    query_scaled = jnp.sum(query_wide[:H], axis=0, keepdims=True) * scale
    query_a = query_wide.astype(BF16).astype(F32)
    query_b = (query_wide - query_a).astype(BF16).astype(F32)
    query_c = query_wide - query_a - query_b
    query_all_parts = jnp.concatenate([query_a, query_b, query_c], axis=0).astype(BF16)
    bias_wide[...] = bias[...].astype(F32).reshape(var_local, 1, D)
    pair_shape = (PAIR, patches, vp)
    pair_rows = PAIR * patches
    weight_load.wait()

    def pair_mask(g):
        return PAIR * g + iota(pair_shape, 0) == iota(pair_shape, 2) // P_SIZE

    def embed(g, carry):
        own = jnp.where(pair_mask(g), pix[None], 0.0).reshape(pair_rows, vp).astype(BF16)
        pair = pl.ds(PAIR * g, PAIR)
        projected = nn(own, weight_in[...]).reshape(PAIR, patches, D)
        low = (projected + bias_wide[pair]).astype(BF16)
        emb[pair] = low
        parts = nt(low.reshape(pair_rows, D), query_all_parts)
        scores[pair] = (
            (parts[:, :COPIES] + parts[:, COPIES : 2 * COPIES] + parts[:, 2 * COPIES :]) * scale
        ).reshape(PAIR, patches, COPIES)
        return carry

    lax.fori_loop(0, var_local // PAIR, embed, 0)
    each_var(lambda p: swap_copy(p, p, p, p).wait_recv())
    for part in range(n_vars):
        up[:, part * width : (part + 1) * width] = nn(take, arrived[part])

    peak = jnp.max(scores[...], axis=0)

    def gather(g, carry):
        total, inner, mixed = carry
        pair = pl.ds(PAIR * g, PAIR)
        values = emb[pair].astype(F32)
        high, low = split_two((up[...][None] * values).reshape(pair_rows, D))
        grad = (nt(high, spread) + nt(low, spread)).reshape(PAIR, patches, COPIES)
        attn_grad[pair] = grad
        power = jnp.exp(scores[pair] - peak[None])
        scores[pair] = power
        wide = expand(power.reshape(pair_rows, COPIES), spread).reshape(PAIR, patches, D)
        return (
            total + jnp.sum(power, axis=0),
            inner + jnp.sum(power * grad, axis=0),
            mixed + jnp.sum(wide * values, axis=0),
        )

    nothing = jnp.zeros((patches, COPIES), F32)
    total, inner, mixed = lax.fori_loop(
        0, var_local // PAIR, gather, (nothing, nothing, jnp.zeros((patches, D), F32))
    )
    stat[mine, 0] = peak
    stat[mine, 1] = total
    stat[mine, 2] = inner
    for part in range(n_vars):
        mix_send[part] = mixed[:, part * width : (part + 1) * width]

    def stat_copy(part, sem_s, sem_r, p):
        return copy(stat.at[part], stat.at[part], st_s.at[sem_s], st_r.at[sem_r], var_dev(p))

    def mix_copy(part, slot, sem_s, sem_r, p):
        return copy(
            mix_send.at[part], mix_recv.at[slot], mx_s.at[sem_s], mx_r.at[sem_r], var_dev(p)
        )

    each_var(lambda p: stat_copy(mine, p, mine, p).start())
    each_var(lambda p: mix_copy(p, mine, p, mine, p).start())
    mix_recv[mine] = mix_send[mine]
    each_var(lambda p: stat_copy(p, p, p, p).wait_recv())
    peak_all = stat[0, 0]
    for part in range(1, n_vars):
        peak_all = jnp.maximum(peak_all, stat[part, 0])
    factors = [jnp.exp(stat[part, 0] - peak_all) for part in range(n_vars)]
    total_all = sum(stat[part, 1] * factors[part] for part in range(n_vars))
    inner_all = sum(stat[part, 2] * factors[part] for part in range(n_vars)) / total_all
    own_factor = jnp.exp(peak - peak_all) / total_all

    each_var(lambda p: mix_copy(p, p, p, p, p).wait_recv())
    mixture = sum(
        expand(factors[part] / total_all, own_spread) * mix_recv[part] for part in range(n_vars)
    )
    tok_send[...] = nn(put, mixture.astype(BF16)).astype(BF16)

    def tok_copy(src_row, dst_row, send, recv, p):
        return copy(
            tok_send.at[aligned(src_row, depth), :], tok_out.at[aligned(dst_row, depth), :],
            tk_s.at[send], tk_r.at[recv], row_dev(p),
        )

    each_row(lambda p: tok_copy(p, me, p, me, p).start())
    tok_out[aligned(me, depth), :] = tok_send[aligned(me, depth), :]

    def part_copy(slot, from_place, line, to_place):
        return copy(
            part_send.at[slot], part_recv.at[from_place, line],
            pt_s.at[slot], pt_r.at[from_place, line], row_dev(my_line * PLANE + to_place),
        )

    per_group = D // LANE // tiles
    per_pair = PAIR * P_SIZE // SUB * per_group
    pair_pixels = PAIR * P_SIZE

    def backward(i, carry):
        pix_grad, query_sum = carry
        g = lax.rem(i + my_line + 1, var_local // PAIR)
        pair = pl.ds(PAIR * g, PAIR)
        values = emb[pair].astype(F32)
        attention = scores[pair] * own_factor[None]
        score_grad = attention * (attn_grad[pair] - inner_all[None])
        both = jnp.concatenate(
            [attention.reshape(pair_rows, COPIES), score_grad.reshape(pair_rows, COPIES)], axis=0
        )
        wide = expand(both, spread)
        attention_wide = wide[:pair_rows].reshape(PAIR, patches, D)
        score_wide = wide[pair_rows:].reshape(PAIR, patches, D)
        grad = attention_wide * up[...][None] + score_wide * query_scaled[None]
        low = grad.astype(BF16).reshape(pair_rows, D)
        bias_sum[pair] = jnp.sum(grad, axis=1, keepdims=True)
        query_sum = query_sum + jnp.sum(jnp.sum(score_wide * values, axis=0), axis=0, keepdims=True)
        rows = pix_t[aligned(g, pair_pixels), :].astype(F32)
        doubled = jnp.concatenate([rows] * PAIR, axis=1)
        kept = iota(doubled.shape, 0) // P_SIZE == iota(doubled.shape, 1) // patches
        found = nn(jnp.where(kept, doubled, 0.0).astype(BF16), low)
        for group in range(pair_pixels // SUB):
            for lane in range(D // LANE):
                slot = g * per_pair + group * per_group + lane // tiles
                part_send[slot, lane % tiles] = found[
                    group * SUB : (group + 1) * SUB, lane * LANE : (lane + 1) * LANE
                ]
        for step in range(per_pair):
            slot = g * per_pair + step
            place = lax.rem(slot, PLANE)

            @pl.when(place != my_place)
            def _():
                part_copy(slot, my_place, slot // PLANE, place).start()

        returned = nt(low, weight_in[...]).reshape(pair_shape)
        pix_grad = pix_grad + jnp.sum(jnp.where(pair_mask(g), returned, 0.0), axis=0)
        return pix_grad, query_sum

    pix_grad, query_sum = lax.fori_loop(
        0, var_local // PAIR, backward, (jnp.zeros((patches, vp), F32), jnp.zeros((1, D), F32))
    )
    for line in range(lines):
        part_recv[my_place, line] = part_send[line * PLANE + my_place]

    query_part[mine] = jnp.broadcast_to(query_sum * scale, (SUB, D))

    def query_copy(part, sem_s, sem_r, p):
        return copy(
            query_part.at[part], query_part.at[part], qp_s.at[sem_s], qp_r.at[sem_r], var_dev(p)
        )

    each_var(lambda p: query_copy(mine, p, mine, p).start())

    grad_t = pix_grad.T.astype(BF16)
    pick = (iota((var_local, vp), 0) == iota((var_local, vp), 1) // P_SIZE).astype(F32).astype(BF16)

    small_send[...] = jnp.zeros_like(small_send)
    bias_tiles = var_local // SUB * (D // LANE)
    for group in range(var_local // SUB):
        rows = jnp.concatenate([bias_sum[group * SUB + k] for k in range(SUB)], axis=0)
        for lane in range(D // LANE):
            number = group * (D // LANE) + lane
            small_send[number % PLANE, number // PLANE] = rows[:, lane * LANE : (lane + 1) * LANE]
    each_var(lambda p: query_copy(p, p, p, p).wait_recv())
    query_all = query_part[0]
    for part in range(1, n_vars):
        query_all = query_all + query_part[part]
    for lane in range(D // LANE):
        number = bias_tiles + lane
        small_send[number % PLANE, number // PLANE] = query_all[:, lane * LANE : (lane + 1) * LANE]

    def small_copy(to_place, from_place, send, recv, p):
        return copy(
            small_send.at[to_place], small_recv.at[from_place], sm_s.at[send], sm_r.at[recv],
            row_dev(my_line * PLANE + p),
        )

    each_place(lambda p: small_copy(p, my_place, p, my_place, p).start())
    small_recv[my_place] = small_send[my_place]

    def field_block(b, carry):
        values = nn(grad_t, placing(b))
        kept = jnp.where(own_pixel((vp, block_pixels), 0), values, 0.0).astype(BF16)
        by_pixel = nn(pick, kept).astype(BF16)
        field_out[:, aligned(b, PTS_BLK)] = nt(by_pixel, matrix[b])
        return carry

    lax.fori_loop(0, blocks, field_block, 0)

    each_place(lambda p: small_copy(p, p, p, p, p).wait_recv())

    def line_copy(to_line, from_line, p):
        return copy(
            plane_sum.at[to_line], line_recv.at[from_line], ln_s.at[to_line], ln_r.at[from_line],
            row_dev(p * PLANE + my_place),
        )

    def plane_total(line):
        each_place(lambda p: part_copy(p, p, line, p).wait_recv())
        part_total, small_total = part_recv[0, line], small_recv[0, line]
        for place in range(1, PLANE):
            part_total = part_total + part_recv[place, line]
            small_total = small_total + small_recv[place, line]
        plane_sum[line, 0:tiles] = part_total
        plane_sum[line, tiles] = small_total

    def send_line(line):
        plane_total(line)
        line_copy(line, my_line, line).start()

    each_line(send_line)
    plane_total(my_line)
    line_recv[my_line] = plane_sum[my_line]
    each_line(lambda p: line_copy(p, p, p).wait_recv())
    done[my_line, my_place] = jnp.sum(line_recv[...], axis=0)

    def up_copy(line, send, recv, p):
        return copy(
            done.at[line, my_place], done.at[line, my_place], up_s.at[send], up_r.at[recv],
            row_dev(p * PLANE + my_place),
        )

    def done_copy(line, place, to_place):
        return copy(
            done.at[line, place], done.at[line, place], dn_s.at[line, to_place],
            dn_r.at[line, place], row_dev(my_line * PLANE + to_place),
        )

    each_line(lambda p: up_copy(my_line, p, my_line, p).start())
    each_place(lambda p: done_copy(my_line, my_place, p).start())

    def pass_on(line):
        up_copy(line, line, line, line).wait_recv()
        each_place(lambda p: done_copy(line, my_place, p).start())

    each_line(pass_on)
    for line in range(lines):
        each_place(lambda p: done_copy(line, p, p).wait_recv())

    each_row(lambda p: tok_copy(p, p, p, p, p).wait_recv())
    each_row(lambda p: og_copy(p, me, p, me, p).wait_send())
    each_row(lambda p: tok_copy(p, me, p, me, p).wait_send())
    for line in range(lines):
        each_place(lambda p: part_copy(line * PLANE + p, my_place, line, p).wait_send())
        each_place(lambda p: done_copy(line, my_place, p).wait_send())
    each_place(lambda p: small_copy(p, my_place, p, my_place, p).wait_send())
    each_line(lambda p: line_copy(p, my_line, p).wait_send())
    each_line(lambda p: up_copy(my_line, p, my_line, p).wait_send())
    each_var(lambda p: swap_copy(mine, p, mine, p).wait_send())
    each_var(lambda p: stat_copy(mine, p, mine, p).wait_send())
    each_var(lambda p: mix_copy(p, mine, p, mine, p).wait_send())
    each_var(lambda p: query_copy(mine, p, mine, p).wait_send())


def finish(
    n_rows, tiles, bias_tiles, tok_in, field_in, done,
    tok_out, field_out, weight_out, bias_out, query_out,
):
    tok_out[...] = tok_in[...]
    field_out[...] = field_in[...]
    across = D // LANE
    for number in range(n_rows * tiles):
        slot, tile = number // tiles, number % tiles
        group, lane = number // across, number % across
        weight_out[group * SUB : (group + 1) * SUB, lane * LANE : (lane + 1) * LANE] = done[
            slot // PLANE, slot % PLANE, tile
        ]
    for number in range(bias_tiles):
        group, lane = number // across, number % across
        bias_out[group * SUB : (group + 1) * SUB, lane * LANE : (lane + 1) * LANE] = done[
            number // PLANE, number % PLANE, tiles
        ]
    for lane in range(across):
        number = bias_tiles + lane
        row = done[number // PLANE, number % PLANE, tiles]
        for half in range(LANE // DH):
            head = lane * (LANE // DH) + half
            query_out[head : head + 1, :] = row[0:1, half * DH : (half + 1) * DH]


def local(
    fields, stencil, stencil_weight, owner_map, embed_weight, embed_bias, agg_query, out_grad
):
    n_rows = lax.axis_size("rows")
    n_vars = lax.axis_size("vars")
    var_local, points = fields.shape
    blocks = points // PTS_BLK
    patches = owner_map.shape[0]
    capacity = out_grad.shape[0]
    slot_depth = capacity // n_rows
    depth = -(-slot_depth // 16) * 16
    vp = var_local * P_SIZE
    width = D // n_vars
    slots = n_rows * depth
    tiles = vp // SUB * (D // LANE) // n_rows
    if depth != slot_depth:
        out_grad = jnp.pad(
            out_grad.reshape(n_rows, slot_depth, D), ((0, 0), (0, depth - slot_depth), (0, 0))
        ).reshape(slots, D)
    vmem = pl.BlockSpec(memory_space=pltpu.VMEM)
    dma = pltpu.SemaphoreType.DMA
    row_sem, var_sem = dma((n_rows,)), dma((n_vars,))
    lines = n_rows // PLANE
    shapes = (
        jax.ShapeDtypeStruct((slots, width), BF16),
        jax.ShapeDtypeStruct((var_local, points), F32),
    )
    tokens, field_grad, done = pl.pallas_call(
        functools.partial(kernel, n_rows, n_vars, var_local, blocks, depth),
        out_shape=shapes
        + (jax.ShapeDtypeStruct((lines, PLANE, tiles + 1, SUB, LANE), F32),),
        in_specs=[vmem] * 5 + [pl.BlockSpec(memory_space=pl.ANY)] + [vmem] * 2
        + [pl.BlockSpec(memory_space=pl.ANY)],
        out_specs=(vmem,) * 3,
        scratch_shapes=[
            pltpu.VMEM((vp, D), BF16),
            pltpu.VMEM((n_vars, slots, width), BF16),
            pltpu.VMEM((blocks, PTS_BLK, PB * P_SIZE), BF16),
            pltpu.VMEM((vp, PTS_BLK), BF16),
            pltpu.VMEM((patches, D), F32),
            pltpu.VMEM((vp, patches), BF16),
            pltpu.VMEM((var_local, patches, D), BF16),
            pltpu.VMEM((var_local, 1, D), F32),
            pltpu.VMEM((var_local, patches, COPIES), F32),
            pltpu.VMEM((var_local, patches, COPIES), F32),
            pltpu.VMEM((n_vars, patches, width), F32),
            pltpu.VMEM((n_vars, patches, width), F32),
            pltpu.VMEM((n_vars, 3, patches, COPIES), F32),
            pltpu.VMEM((slots, width), BF16),
            pltpu.VMEM((var_local, 1, D), F32),
            pltpu.VMEM((n_vars, SUB, D), F32),
            pltpu.VMEM((n_rows, tiles, SUB, LANE), F32),
            pltpu.VMEM((PLANE, lines, tiles, SUB, LANE), F32),
            pltpu.VMEM((PLANE, lines, SUB, LANE), F32),
            pltpu.VMEM((PLANE, lines, SUB, LANE), F32),
            pltpu.VMEM((lines, tiles + 1, SUB, LANE), F32),
            pltpu.VMEM((lines, tiles + 1, SUB, LANE), F32),
        ]
        + [row_sem] * 2 + [var_sem] * 6 + [row_sem] * 2 + [var_sem] * 2
        + [row_sem, dma((PLANE, lines))] + [dma((PLANE,))] * 2 + [dma((lines,))] * 4
        + [dma((lines, PLANE))] * 2 + [dma((2,))],
        compiler_params=pltpu.CompilerParams(
            collective_id=0, has_side_effects=True, vmem_limit_bytes=56 * 1024 * 1024
        ),
        name="encoder",
    )(
        fields,
        stencil.T,
        stencil_weight.T,
        owner_map,
        owner_map.reshape(1, patches),
        embed_weight.reshape(vp, D),
        embed_bias,
        agg_query,
        out_grad,
    )
    tokens, field_grad, weight_grad, bias_grad, query_grad = pl.pallas_call(
        functools.partial(finish, n_rows, tiles, var_local // SUB * (D // LANE)),
        out_shape=shapes
        + (
            jax.ShapeDtypeStruct((vp, D), F32),
            jax.ShapeDtypeStruct((var_local, D), F32),
            jax.ShapeDtypeStruct((H, DH), F32),
        ),
        in_specs=[vmem] * 3,
        out_specs=(vmem,) * 5,
        compiler_params=pltpu.CompilerParams(vmem_limit_bytes=32 * 1024 * 1024),
        name="finish",
    )(tokens, field_grad, done)
    if depth != slot_depth:
        tokens = tokens.reshape(n_rows, depth, width)[:, :slot_depth].reshape(capacity, width)
    return tokens, field_grad, weight_grad.reshape(var_local, P_SIZE, D), bias_grad, query_grad


def solution(mesh):
    return jax.shard_map(
        local,
        mesh=mesh,
        in_specs=(
            P("vars", "rows"),
            P("rows", None),
            P("rows", None),
            P("rows", None),
            P("vars", None, None),
            P("vars", None),
            P(),
            P("rows", None),
        ),
        out_specs=(
            P("rows", "vars"),
            P("vars", "rows"),
            P("vars", None, None),
            P("vars", None),
            P(),
        ),
        check_vma=False,
    )
```

```python
import functools
import math

import jax
import jax.numpy as jnp
from jax import lax
from jax.experimental import pallas as pl
from jax.experimental.pallas import tpu as pltpu
from jax.sharding import PartitionSpec as P

D = 1024
H = 16
DH = 64
P_SIZE = 16
K = 4
PTS_BLK = 1024
PB = 32
LANE = 128
SUB = 8
J_STEP = 64
PLANE = 4
PAIR = 2
COPIES = 2 * H
MESH = pl.DeviceIdType.MESH
F32 = jnp.float32
BF16 = jnp.bfloat16


def nn(a, b):
    return lax.dot_general(a, b, (((1,), (0,)), ((), ())), preferred_element_type=F32)


def nt(a, b):
    return lax.dot_general(a, b, (((1,), (1,)), ((), ())), preferred_element_type=F32)


def iota(shape, axis):
    return lax.broadcasted_iota(jnp.int32, shape, axis)


def split_two(x):
    high = x.astype(BF16)
    return high, (x - high.astype(F32)).astype(BF16)


def packed(x):
    high = x.astype(BF16).astype(F32)
    return jnp.where(iota(x.shape, 1) < H, high, x - high).astype(BF16)


def expand(x, spread):
    return nn(packed(x), spread)


def aligned(start, size):
    return pl.ds(pl.multiple_of(start * size, size), size)


def kernel(
    n_rows, n_vars, var_local, blocks, depth,
    fields, stencil, stencil_weight, owner_col, owner_row, weight, bias, query, out_grad,
    tok_out, field_out, done,
    weight_in, arrived, matrix, spread_fields, up, pix_t, emb, bias_wide, scores, attn_grad,
    mix_send, mix_recv, stat, tok_send, bias_sum, query_part, part_send, part_recv,
    small_send, small_recv, plane_sum, line_recv, small_sum, small_line,
    og_s, og_r, sw_s, sw_r, mx_s, mx_r, st_s, st_r, tk_s, tk_r, qp_s, qp_r,
    pt_s, pt_r, sm_s, sm_r, ln_s, ln_r, sl_s, sl_r, up_s, up_r, dn_s, dn_r, load_sem,
):
    me = lax.axis_index("rows")
    mine = lax.axis_index("vars")
    lines = n_rows // PLANE
    my_line, my_place = me // PLANE, lax.rem(me, PLANE)
    patches = blocks * PB
    vp = var_local * P_SIZE
    width = D // n_vars
    slots = n_rows * depth
    block_pixels = PB * P_SIZE
    scale = 1.0 / math.sqrt(DH)
    tiles = vp // SUB * (D // LANE) // n_rows

    def row_dev(peer):
        return (peer, mine)

    def var_dev(peer):
        return (me, peer)

    def copy(src, dst, send, recv, device):
        return pltpu.make_async_remote_copy(
            src_ref=src, dst_ref=dst, send_sem=send, recv_sem=recv,
            device_id=device, device_id_type=MESH,
        )

    def each_row(body):
        def step(i, carry):
            body(lax.rem(me + i, n_rows))
            return carry

        lax.fori_loop(1, n_rows, step, 0)

    def each_var(body):
        for i in range(1, n_vars):
            body(lax.rem(mine + i, n_vars))

    def each_place(body):
        for i in range(1, PLANE):
            body(lax.rem(my_place + i, PLANE))

    def each_line(body):
        for i in range(1, lines):
            body(lax.rem(my_line + i, lines))

    own_lanes = pl.ds(pl.multiple_of(mine * width, LANE), width)
    weight_load = pltpu.make_async_copy(weight, weight_in, load_sem.at[0])
    weight_load.start()
    own_load = pltpu.make_async_copy(
        out_grad.at[aligned(me, depth), own_lanes],
        arrived.at[mine, aligned(me, depth), :],
        load_sem.at[1],
    )
    own_load.start()
    barrier = pltpu.get_barrier_semaphore()
    each_row(
        lambda p: pl.semaphore_signal(barrier, inc=1, device_id=row_dev(p), device_id_type=MESH)
    )
    each_var(
        lambda p: pl.semaphore_signal(barrier, inc=1, device_id=var_dev(p), device_id_type=MESH)
    )

    def og_copy(src_row, dst_row, send, recv, p):
        return copy(
            out_grad.at[aligned(src_row, depth), own_lanes],
            arrived.at[mine, aligned(dst_row, depth), :],
            og_s.at[send], og_r.at[recv], row_dev(p),
        )


    def own_pixel(shape, row_axis):
        return iota(shape, 0) % P_SIZE == iota(shape, 1) % P_SIZE

    def placing(b):
        shape = (patches, block_pixels)
        return (iota(shape, 0) == b * PB + iota(shape, 1) // P_SIZE).astype(F32).astype(BF16)

    def interp(b, pix):
        columns = aligned(b, block_pixels)
        index_rows = stencil[:, columns]
        weight_rows = stencil_weight[:, columns]

        def chunk(j, carry):
            points = j * J_STEP + iota((J_STEP, block_pixels), 0)
            total = jnp.zeros((J_STEP, block_pixels), F32)
            for entry in range(K):
                total = total + jnp.where(
                    index_rows[entry : entry + 1] == points,
                    weight_rows[entry : entry + 1],
                    0.0,
                )
            matrix[b, aligned(j, J_STEP), :] = total.astype(BF16)
            return carry

        lax.fori_loop(0, PTS_BLK // J_STEP, chunk, 0)
        block_fields = fields[:, aligned(b, PTS_BLK)].astype(F32)
        for v in range(var_local):
            spread_fields[v * P_SIZE : (v + 1) * P_SIZE, :] = jnp.broadcast_to(
                block_fields[v : v + 1], (P_SIZE, PTS_BLK)
            ).astype(BF16)
        values = nn(spread_fields[...], matrix[b]).astype(BF16).astype(F32)
        kept = jnp.where(own_pixel((vp, block_pixels), 0), values, 0.0).astype(BF16)
        return pix + nt(placing(b), kept)

    pix = interp(0, jnp.zeros((patches, vp), F32))
    pl.semaphore_wait(barrier, n_rows + n_vars - 2)
    each_row(lambda p: og_copy(p, me, p, me, p).start())
    pix = lax.fori_loop(1, blocks, interp, pix)
    pix_t[...] = pix.T.astype(BF16)

    square = (patches, patches)
    same = owner_col[...] == owner_row[...]
    rank_col = jnp.sum(
        jnp.where(same & (iota(square, 1) < iota(square, 0)), 1.0, 0.0), axis=1, keepdims=True
    ).astype(jnp.int32)
    rank_row = jnp.sum(
        jnp.where(same & (iota(square, 0) < iota(square, 1)), 1.0, 0.0), axis=0, keepdims=True
    ).astype(jnp.int32)
    slot_col = owner_col[...] * depth + rank_col
    slot_row = owner_row[...] * depth + rank_row
    take = (slot_col == iota((patches, slots), 1)).astype(F32).astype(BF16)
    put = (slot_row == iota((slots, patches), 0)).astype(F32).astype(BF16)

    own_load.wait()
    each_row(lambda p: og_copy(p, p, p, p, p).wait_recv())

    def swap_copy(part, sem_s, sem_r, p):
        return copy(arrived.at[part], arrived.at[part], sw_s.at[sem_s], sw_r.at[sem_r], var_dev(p))

    each_var(lambda p: swap_copy(mine, p, mine, p).start())

    heads = iota((COPIES, D), 0) % H == iota((COPIES, D), 1) // DH
    spread = heads.astype(F32).astype(BF16)
    own_head = (mine * width + iota((COPIES, width), 1)) // DH
    own_spread = (iota((COPIES, width), 0) % H == own_head).astype(F32).astype(BF16)
    query_tiled = jnp.concatenate([query[...]] * H, axis=1)
    query_wide = jnp.where(heads, jnp.concatenate([query_tiled] * 2, axis=0), 0.0)
    query_scaled = jnp.sum(query_wide[:H], axis=0, keepdims=True) * scale
    query_a = query_wide.astype(BF16).astype(F32)
    query_b = (query_wide - query_a).astype(BF16).astype(F32)
    query_c = query_wide - query_a - query_b
    query_all_parts = jnp.concatenate([query_a, query_b, query_c], axis=0).astype(BF16)
    bias_wide[...] = bias[...].astype(F32).reshape(var_local, 1, D)
    pair_shape = (PAIR, patches, vp)
    pair_rows = PAIR * patches
    weight_load.wait()

    def pair_mask(g):
        return PAIR * g + iota(pair_shape, 0) == iota(pair_shape, 2) // P_SIZE

    def embed(g, carry):
        own = jnp.where(pair_mask(g), pix[None], 0.0).reshape(pair_rows, vp).astype(BF16)
        pair = pl.ds(PAIR * g, PAIR)
        projected = nn(own, weight_in[...]).reshape(PAIR, patches, D)
        low = (projected + bias_wide[pair]).astype(BF16)
        emb[pair] = low
        parts = nt(low.reshape(pair_rows, D), query_all_parts)
        scores[pair] = (
            (parts[:, :COPIES] + parts[:, COPIES : 2 * COPIES] + parts[:, 2 * COPIES :]) * scale
        ).reshape(PAIR, patches, COPIES)
        return carry

    lax.fori_loop(0, var_local // PAIR, embed, 0)
    each_var(lambda p: swap_copy(p, p, p, p).wait_recv())
    for part in range(n_vars):
        up[:, part * width : (part + 1) * width] = nn(take, arrived[part])

    peak = jnp.max(scores[...], axis=0)

    def weigh(g, carry):
        total, inner = carry
        pair = pl.ds(PAIR * g, PAIR)
        values = emb[pair].astype(F32)
        high, low = split_two((up[...][None] * values).reshape(pair_rows, D))
        grad = (nt(high, spread) + nt(low, spread)).reshape(PAIR, patches, COPIES)
        attn_grad[pair] = grad
        power = jnp.exp(scores[pair] - peak[None])
        scores[pair] = power
        return total + jnp.sum(power, axis=0), inner + jnp.sum(power * grad, axis=0)

    nothing = jnp.zeros((patches, COPIES), F32)
    total, inner = lax.fori_loop(0, var_local // PAIR, weigh, (nothing, nothing))
    stat[mine, 0] = peak
    stat[mine, 1] = total
    stat[mine, 2] = inner

    def stat_copy(part, sem_s, sem_r, p):
        return copy(stat.at[part], stat.at[part], st_s.at[sem_s], st_r.at[sem_r], var_dev(p))

    def mix_copy(part, slot, sem_s, sem_r, p):
        return copy(
            mix_send.at[part], mix_recv.at[slot], mx_s.at[sem_s], mx_r.at[sem_r], var_dev(p)
        )

    each_var(lambda p: stat_copy(mine, p, mine, p).start())

    def mix(g, mixed):
        pair = pl.ds(PAIR * g, PAIR)
        wide = expand(scores[pair].reshape(pair_rows, COPIES), spread)
        return mixed + jnp.sum(
            wide.reshape(PAIR, patches, D) * emb[pair].astype(F32), axis=0
        )

    mixed = lax.fori_loop(0, var_local // PAIR, mix, jnp.zeros((patches, D), F32))
    for part in range(n_vars):
        mix_send[part] = mixed[:, part * width : (part + 1) * width]
    each_var(lambda p: mix_copy(p, mine, p, mine, p).start())
    mix_recv[mine] = mix_send[mine]
    each_var(lambda p: stat_copy(p, p, p, p).wait_recv())
    peak_all = stat[0, 0]
    for part in range(1, n_vars):
        peak_all = jnp.maximum(peak_all, stat[part, 0])
    factors = [jnp.exp(stat[part, 0] - peak_all) for part in range(n_vars)]
    total_all = sum(stat[part, 1] * factors[part] for part in range(n_vars))
    inner_all = sum(stat[part, 2] * factors[part] for part in range(n_vars)) / total_all
    own_factor = jnp.exp(peak - peak_all) / total_all

    def part_copy(slot, from_place, line, to_place):
        return copy(
            part_send.at[slot], part_recv.at[from_place, line],
            pt_s.at[slot], pt_r.at[from_place, line], row_dev(my_line * PLANE + to_place),
        )

    per_group = D // LANE // tiles
    per_pair = PAIR * P_SIZE // SUB * per_group
    pair_pixels = PAIR * P_SIZE

    pair_lines = per_pair // PLANE

    def turn(i):
        return lax.rem(i + my_line + 1, var_local // PAIR)

    def line_copy(to_line, from_line, p):
        return copy(
            plane_sum.at[to_line], line_recv.at[from_line], ln_s.at[to_line], ln_r.at[from_line],
            row_dev(p * PLANE + my_place),
        )

    def plane_total(line):
        each_place(lambda p: part_copy(p, p, line, p).wait_recv())
        part_total = part_recv[0, line]
        for place in range(1, PLANE):
            part_total = part_total + part_recv[place, line]
        plane_sum[line] = part_total

    def send_lines(i):
        for k in range(pair_lines):
            line = turn(i) * pair_lines + k

            @pl.when(line != my_line)
            def _():
                plane_total(line)
                line_copy(line, my_line, line).start()

    def backward(i, carry):
        pix_grad, query_sum = carry
        g = turn(i)
        pair = pl.ds(PAIR * g, PAIR)
        attention = scores[pair] * own_factor[None]
        score_grad = attention * (attn_grad[pair] - inner_all[None])
        both = jnp.concatenate(
            [attention.reshape(pair_rows, COPIES), score_grad.reshape(pair_rows, COPIES)], axis=0
        )
        both = packed(both)
        wide = nn(both, spread)
        attention_wide = wide[:pair_rows].reshape(PAIR, patches, D)
        score_wide = wide[pair_rows:].reshape(PAIR, patches, D)
        grad = attention_wide * up[...][None] + score_wide * query_scaled[None]
        low = grad.astype(BF16).reshape(pair_rows, D)
        bias_sum[pair] = jnp.sum(grad, axis=1, keepdims=True)
        query_sum = query_sum + lax.dot_general(
            both[pair_rows:], emb[pair].reshape(pair_rows, D), (((0,), (0,)), ((), ())),
            preferred_element_type=F32,
        )
        rows = pix_t[aligned(g, pair_pixels), :].astype(F32)
        doubled = jnp.concatenate([rows] * PAIR, axis=1)
        kept = iota(doubled.shape, 0) // P_SIZE == iota(doubled.shape, 1) // patches
        found = nn(jnp.where(kept, doubled, 0.0).astype(BF16), low)
        for group in range(pair_pixels // SUB):
            for lane in range(D // LANE):
                slot = g * per_pair + group * per_group + lane // tiles
                part_send[slot, lane % tiles] = found[
                    group * SUB : (group + 1) * SUB, lane * LANE : (lane + 1) * LANE
                ]
        for step in range(per_pair):
            slot = g * per_pair + step
            place = lax.rem(slot, PLANE)

            @pl.when(place != my_place)
            def _():
                part_copy(slot, my_place, slot // PLANE, place).start()

        returned = nt(low, weight_in[...]).reshape(pair_shape)
        pix_grad = pix_grad + jnp.sum(jnp.where(pair_mask(g), returned, 0.0), axis=0)
        for k in range(pair_lines):
            line = g * pair_lines + k
            part_recv[my_place, line] = part_send[line * PLANE + my_place]

        if not isinstance(i, int):
            send_lines(i - 1)
        return pix_grad, query_sum

    sums = backward(0, (jnp.zeros((patches, vp), F32), jnp.zeros((COPIES, D), F32)))
    each_var(lambda p: mix_copy(p, p, p, p, p).wait_recv())
    mixture = sum(
        expand(factors[part] / total_all, own_spread) * mix_recv[part] for part in range(n_vars)
    )
    tok_send[...] = nn(put, mixture.astype(BF16)).astype(BF16)

    def tok_copy(src_row, dst_row, send, recv, p):
        return copy(
            tok_send.at[aligned(src_row, depth), :], tok_out.at[aligned(dst_row, depth), :],
            tk_s.at[send], tk_r.at[recv], row_dev(p),
        )

    each_row(lambda p: tok_copy(p, me, p, me, p).start())
    tok_out[aligned(me, depth), :] = tok_send[aligned(me, depth), :]

    pix_grad, query_rows = lax.fori_loop(1, var_local // PAIR, backward, sums)
    query_sum = jnp.sum(jnp.where(heads, query_rows, 0.0), axis=0, keepdims=True)
    query_part[mine] = jnp.broadcast_to(query_sum * scale, (SUB, D))

    def query_copy(part, sem_s, sem_r, p):
        return copy(
            query_part.at[part], query_part.at[part], qp_s.at[sem_s], qp_r.at[sem_r], var_dev(p)
        )

    each_var(lambda p: query_copy(mine, p, mine, p).start())

    grad_t = pix_grad.T.astype(BF16)
    pick = (iota((var_local, vp), 0) == iota((var_local, vp), 1) // P_SIZE).astype(F32).astype(BF16)

    small_send[...] = jnp.zeros_like(small_send)
    bias_tiles = var_local // SUB * (D // LANE)
    for group in range(var_local // SUB):
        rows = jnp.concatenate([bias_sum[group * SUB + k] for k in range(SUB)], axis=0)
        for lane in range(D // LANE):
            number = group * (D // LANE) + lane
            small_send[number % PLANE, number // PLANE] = rows[:, lane * LANE : (lane + 1) * LANE]
    each_var(lambda p: query_copy(p, p, p, p).wait_recv())
    query_all = query_part[0]
    for part in range(1, n_vars):
        query_all = query_all + query_part[part]
    for lane in range(D // LANE):
        number = bias_tiles + lane
        small_send[number % PLANE, number // PLANE] = query_all[:, lane * LANE : (lane + 1) * LANE]

    def small_copy(to_place, from_place, send, recv, p):
        return copy(
            small_send.at[to_place], small_recv.at[from_place], sm_s.at[send], sm_r.at[recv],
            row_dev(my_line * PLANE + p),
        )

    each_place(lambda p: small_copy(p, my_place, p, my_place, p).start())
    small_recv[my_place] = small_send[my_place]

    def field_block(b, carry):
        values = nn(grad_t, placing(b))
        kept = jnp.where(own_pixel((vp, block_pixels), 0), values, 0.0).astype(BF16)
        by_pixel = nn(pick, kept).astype(BF16)
        field_out[:, aligned(b, PTS_BLK)] = nt(by_pixel, matrix[b])
        return carry

    send_lines(var_local // PAIR - 1)
    plane_total(my_line)
    line_recv[my_line] = plane_sum[my_line]
    lax.fori_loop(0, blocks // 2, field_block, 0)
    each_place(lambda p: small_copy(p, p, p, p, p).wait_recv())
    small_sum[...] = jnp.sum(small_recv[...], axis=0)

    def small_line_copy(to_line, from_line, p):
        return copy(
            small_sum.at[to_line], small_line.at[from_line], sl_s.at[to_line],
            sl_r.at[from_line], row_dev(p * PLANE + my_place),
        )

    each_line(lambda p: small_line_copy(p, my_line, p).start())
    small_line[my_line] = small_sum[my_line]
    lax.fori_loop(blocks // 2, blocks, field_block, 0)
    each_line(lambda p: line_copy(p, p, p).wait_recv())
    each_line(lambda p: small_line_copy(p, p, p).wait_recv())
    done[my_line, my_place, 0:tiles] = jnp.sum(line_recv[...], axis=0)
    done[my_line, my_place, tiles] = jnp.sum(small_line[...], axis=0)

    def up_copy(line, send, recv, p):
        return copy(
            done.at[line, my_place], done.at[line, my_place], up_s.at[send], up_r.at[recv],
            row_dev(p * PLANE + my_place),
        )

    def done_copy(line, place, to_place):
        return copy(
            done.at[line, place], done.at[line, place], dn_s.at[line, to_place],
            dn_r.at[line, place], row_dev(my_line * PLANE + to_place),
        )

    each_line(lambda p: up_copy(my_line, p, my_line, p).start())
    each_place(lambda p: done_copy(my_line, my_place, p).start())

    def pass_on(line):
        up_copy(line, line, line, line).wait_recv()
        each_place(lambda p: done_copy(line, my_place, p).start())

    each_line(pass_on)
    for line in range(lines):
        each_place(lambda p: done_copy(line, p, p).wait_recv())

    each_row(lambda p: tok_copy(p, p, p, p, p).wait_recv())
    each_row(lambda p: og_copy(p, me, p, me, p).wait_send())
    each_row(lambda p: tok_copy(p, me, p, me, p).wait_send())
    for line in range(lines):
        each_place(lambda p: part_copy(line * PLANE + p, my_place, line, p).wait_send())
        each_place(lambda p: done_copy(line, my_place, p).wait_send())
    each_place(lambda p: small_copy(p, my_place, p, my_place, p).wait_send())
    each_line(lambda p: line_copy(p, my_line, p).wait_send())
    each_line(lambda p: small_line_copy(p, my_line, p).wait_send())
    each_line(lambda p: up_copy(my_line, p, my_line, p).wait_send())
    each_var(lambda p: swap_copy(mine, p, mine, p).wait_send())
    each_var(lambda p: stat_copy(mine, p, mine, p).wait_send())
    each_var(lambda p: mix_copy(p, mine, p, mine, p).wait_send())
    each_var(lambda p: query_copy(mine, p, mine, p).wait_send())


def finish(
    n_rows, tiles, bias_tiles, tok_in, field_in, done_in,
    tok_out, field_out, weight_out, bias_out, query_out, done, sems,
):
    done_load = pltpu.make_async_copy(done_in, done, sems.at[0])
    tok_move = pltpu.make_async_copy(tok_in, tok_out, sems.at[1])
    field_move = pltpu.make_async_copy(field_in, field_out, sems.at[2])
    done_load.start()
    tok_move.start()
    field_move.start()
    done_load.wait()
    across = D // LANE
    for number in range(n_rows * tiles):
        slot, tile = number // tiles, number % tiles
        group, lane = number // across, number % across
        weight_out[group * SUB : (group + 1) * SUB, lane * LANE : (lane + 1) * LANE] = done[
            slot // PLANE, slot % PLANE, tile
        ]
    for number in range(bias_tiles):
        group, lane = number // across, number % across
        bias_out[group * SUB : (group + 1) * SUB, lane * LANE : (lane + 1) * LANE] = done[
            number // PLANE, number % PLANE, tiles
        ]
    for lane in range(across):
        number = bias_tiles + lane
        row = done[number // PLANE, number % PLANE, tiles]
        for half in range(LANE // DH):
            head = lane * (LANE // DH) + half
            query_out[head : head + 1, :] = row[0:1, half * DH : (half + 1) * DH]
    tok_move.wait()
    field_move.wait()


def local(
    fields, stencil, stencil_weight, owner_map, embed_weight, embed_bias, agg_query, out_grad
):
    n_rows = lax.axis_size("rows")
    n_vars = lax.axis_size("vars")
    var_local, points = fields.shape
    blocks = points // PTS_BLK
    patches = owner_map.shape[0]
    capacity = out_grad.shape[0]
    slot_depth = capacity // n_rows
    depth = -(-slot_depth // 16) * 16
    vp = var_local * P_SIZE
    width = D // n_vars
    slots = n_rows * depth
    tiles = vp // SUB * (D // LANE) // n_rows
    if depth != slot_depth:
        out_grad = jnp.pad(
            out_grad.reshape(n_rows, slot_depth, D), ((0, 0), (0, depth - slot_depth), (0, 0))
        ).reshape(slots, D)
    vmem = pl.BlockSpec(memory_space=pltpu.VMEM)
    dma = pltpu.SemaphoreType.DMA
    row_sem, var_sem = dma((n_rows,)), dma((n_vars,))
    lines = n_rows // PLANE
    shapes = (
        jax.ShapeDtypeStruct((slots, width), BF16),
        jax.ShapeDtypeStruct((var_local, points), F32),
    )
    tokens, field_grad, done = pl.pallas_call(
        functools.partial(kernel, n_rows, n_vars, var_local, blocks, depth),
        out_shape=shapes
        + (jax.ShapeDtypeStruct((lines, PLANE, tiles + 1, SUB, LANE), F32),),
        in_specs=[vmem] * 5 + [pl.BlockSpec(memory_space=pl.ANY)] + [vmem] * 2
        + [pl.BlockSpec(memory_space=pl.ANY)],
        out_specs=(vmem,) * 3,
        scratch_shapes=[
            pltpu.VMEM((vp, D), BF16),
            pltpu.VMEM((n_vars, slots, width), BF16),
            pltpu.VMEM((blocks, PTS_BLK, PB * P_SIZE), BF16),
            pltpu.VMEM((vp, PTS_BLK), BF16),
            pltpu.VMEM((patches, D), F32),
            pltpu.VMEM((vp, patches), BF16),
            pltpu.VMEM((var_local, patches, D), BF16),
            pltpu.VMEM((var_local, 1, D), F32),
            pltpu.VMEM((var_local, patches, COPIES), F32),
            pltpu.VMEM((var_local, patches, COPIES), F32),
            pltpu.VMEM((n_vars, patches, width), F32),
            pltpu.VMEM((n_vars, patches, width), F32),
            pltpu.VMEM((n_vars, 3, patches, COPIES), F32),
            pltpu.VMEM((slots, width), BF16),
            pltpu.VMEM((var_local, 1, D), F32),
            pltpu.VMEM((n_vars, SUB, D), F32),
            pltpu.VMEM((n_rows, tiles, SUB, LANE), F32),
            pltpu.VMEM((PLANE, lines, tiles, SUB, LANE), F32),
            pltpu.VMEM((PLANE, lines, SUB, LANE), F32),
            pltpu.VMEM((PLANE, lines, SUB, LANE), F32),
            pltpu.VMEM((lines, tiles, SUB, LANE), F32),
            pltpu.VMEM((lines, tiles, SUB, LANE), F32),
            pltpu.VMEM((lines, SUB, LANE), F32),
            pltpu.VMEM((lines, SUB, LANE), F32),
        ]
        + [row_sem] * 2 + [var_sem] * 6 + [row_sem] * 2 + [var_sem] * 2
        + [row_sem, dma((PLANE, lines))] + [dma((PLANE,))] * 2 + [dma((lines,))] * 6
        + [dma((lines, PLANE))] * 2 + [dma((2,))],
        compiler_params=pltpu.CompilerParams(
            collective_id=0, has_side_effects=True, vmem_limit_bytes=56 * 1024 * 1024
        ),
        name="encoder",
    )(
        fields,
        stencil.T,
        stencil_weight.T,
        owner_map,
        owner_map.reshape(1, patches),
        embed_weight.reshape(vp, D),
        embed_bias,
        agg_query,
        out_grad,
    )
    tokens, field_grad, weight_grad, bias_grad, query_grad = pl.pallas_call(
        functools.partial(finish, n_rows, tiles, var_local // SUB * (D // LANE)),
        out_shape=shapes
        + (
            jax.ShapeDtypeStruct((vp, D), F32),
            jax.ShapeDtypeStruct((var_local, D), F32),
            jax.ShapeDtypeStruct((H, DH), F32),
        ),
        in_specs=[pl.BlockSpec(memory_space=pl.ANY)] * 3,
        out_specs=(pl.BlockSpec(memory_space=pl.ANY),) * 2 + (vmem,) * 3,
        scratch_shapes=[pltpu.VMEM((lines, PLANE, tiles + 1, SUB, LANE), F32), dma((3,))],
        compiler_params=pltpu.CompilerParams(vmem_limit_bytes=60 * 1024 * 1024),
        name="finish",
    )(tokens, field_grad, done)
    if depth != slot_depth:
        tokens = tokens.reshape(n_rows, depth, width)[:, :slot_depth].reshape(capacity, width)
    return tokens, field_grad, weight_grad.reshape(var_local, P_SIZE, D), bias_grad, query_grad


def solution(mesh):
    return jax.shard_map(
        local,
        mesh=mesh,
        in_specs=(
            P("vars", "rows"),
            P("rows", None),
            P("rows", None),
            P("rows", None),
            P("vars", None, None),
            P("vars", None),
            P(),
            P("rows", None),
        ),
        out_specs=(
            P("rows", "vars"),
            P("vars", "rows"),
            P("vars", None, None),
            P("vars", None),
            P(),
        ),
        check_vma=False,
    )
```
